256 devices in a mesh: region: 32 (over y, z_lo, core), group: 8 (over x, z_hi).
Axes of the slice: x: 4, y: 4, z: 8 (z_hi: 2, z_lo: 4; z = z_hi * 4 + z_lo), core: 2. Of those that a mesh axis runs over, the one named last changes fastest.
Arguments:
- node_latents: bfloat16 [262144, 512], P(('region', 'group')), may hold values from -6 to 6
- edge_latents: bfloat16 [1048576, 512], P(('region', 'group')), may hold values from -6 to 6
- senders: int32 [1048576], P(('region', 'group')), may hold values from 0 to 2559, as said below
- receiver_tile: int32 [8192], P(('region', 'group')), may hold values from 0 to 7
- receiver_row: int32 [1048576], P(('region', 'group')), may hold values from 0 to 127
- edge_mask: int32 [1048576], P(('region', 'group')), may hold values from 0 to 1, as said below
- send_map: int32 [256, 2, 2], replicated, may hold values from 0 to 7, as said below
- w_edge: bfloat16 [512, 512], replicated, may hold values from -0.15625 to 0.15625
- w_send: bfloat16 [512, 512], replicated, may hold values from -0.15625 to 0.15625
- w_recv: bfloat16 [512, 512], replicated, may hold values from -0.15625 to 0.15625
- w_edge_out: bfloat16 [512, 512], replicated, may hold values from -0.25 to 0.25
- w_node: bfloat16 [512, 512], replicated, may hold values from -0.1875 to 0.1875
- w_node_agg: bfloat16 [512, 512], replicated, may hold values from -0.1875 to 0.1875
- w_node_out: bfloat16 [512, 512], replicated, may hold values from -0.25 to 0.25
Outputs:
- new_nodes: bfloat16 [262144, 512], P(('region', 'group'))
- new_edges: bfloat16 [1048576, 512], P(('region', 'group'))
The draws below stay inside these ranges and needn't reach their ends.
Inputs may be any that keep to these rules, and one draw needn't show every extreme that they name: `senders`: rows 0 to 1023 of a sender table are the device's own nodes, then 2 * 128 rows from the lower region, 256 from the upper, then 1024 coarse rows. `send_map`: the 2 tiles of one device and one direction are distinct. `edge_mask`: on each device the live edges come first, at least half of its slots.
All inputs are finite; a program needn't handle non-finite values.
Results may differ from the reference program's by a relative error of at most 0.0054.
Values may be sent and summed in bfloat16 or wider, within the bound.
No kernel may reach another device: no remote copies, remote signals or barrier semaphores. Data moves between devices by JAX's collectives and lax.ppermute only.
A program may use at most 128 MiB of HBM per device.

```python
import jax
import jax.numpy as jnp
from jax import lax

D = 512
TILE = 128
NTILE = 8
CT = 1
SEND = 2
ETILE = 32
PANEL = 1024
EXT = 2560
NODES = 262144
EDGES = 1048576
N_REGION = 32
N_GROUP = 8
DEVICES = 256


def draw_senders(key, part):
    key = jax.random.fold_in(key, 2)
    key_kind, key_local, key_halo, key_panel = jax.random.split(key, 4)
    edge_rows = ETILE * TILE
    shape_all = (DEVICES, edge_rows)
    category = jax.random.randint(key_kind, shape_all, 0, 20)
    local_rows = jax.random.randint(key_local, shape_all, 0, NTILE * TILE)
    halo_pick = NTILE * TILE + jax.random.randint(key_halo, shape_all, 0, 2 * SEND * TILE)
    panel_pick = NTILE * TILE + 2 * SEND * TILE + jax.random.randint(key_panel, shape_all, 0, PANEL)
    picked = jnp.where(category < 12, local_rows, jnp.where(category < 16, halo_pick, panel_pick))
    picked = picked.at[0, 0].set(EXT - 1).at[0, 1].set(0)
    return picked.reshape(-1).astype(jnp.int32)


def draw_edge_mask(key, part):
    key = jax.random.fold_in(key, 3)
    edge_rows = ETILE * TILE
    live_count = jax.random.randint(key, (DEVICES,), edge_rows // 2, edge_rows + 1)
    live_count = live_count.at[0].set(edge_rows)
    positions = jnp.arange(edge_rows, dtype=jnp.int32)
    return (positions[None, :] < live_count[:, None]).astype(jnp.int32).reshape(-1)


def draw_send_map(key, part):
    key = jax.random.fold_in(key, 1)
    scores = jax.random.randint(key, (DEVICES, 2, NTILE), 0, 1 << 20) * NTILE + jnp.arange(NTILE, dtype=jnp.int32)
    scores = scores.at[0, 0, NTILE - 1].add(1 << 28).at[0, 1, 0].add(1 << 28)
    chosen_vals, chosen = jax.lax.top_k(scores, SEND)
    return chosen.astype(jnp.int32)


def with_ends(drawn, stream_key, least, largest):
    index_at = [jax.random.randint(jax.random.fold_in(stream_key, axis), (), 0, length) for axis, length in enumerate(drawn.shape)]
    longest = drawn.shape.index(max(drawn.shape))
    beside = index_at[:longest] + [(index_at[longest] + 1) % drawn.shape[longest]] + index_at[longest + 1:]
    return drawn.at[tuple(index_at)].set(least).at[tuple(beside)].set(largest)


def block_levels(rng, shape, cuts, smallest, largest):
    def one(position, parts):
        draws = jax.random.uniform(jax.random.fold_in(jax.random.fold_in(rng, 6), position), (parts,), jnp.float32, smallest / len(cuts), largest / len(cuts))
        return jnp.repeat(jnp.exp(draws), shape[position] // parts).reshape((-1,) + (1,) * (len(shape) - position - 1))

    factor_of = one(*cuts[0])
    for cut in cuts[1:]:
        factor_of = factor_of * one(*cut)
    return factor_of


def scatter_about(key, extent, width, bound, shards=(), held_as=jnp.bfloat16):
    drawn = width * jax.random.normal(key, extent, jnp.float32)
    if shards:
        drawn = drawn * block_levels(key, extent, shards, -0.22, 0.18)
    return jnp.clip(drawn, -bound, bound).astype(held_as)


def setup_inputs(seed: int = 0) -> dict:
    keys = jax.random.split(jax.random.key(seed), 15)
    return {
        "node_latents": scatter_about(keys[0], (NODES, D), 1.0, 6.0, ((0, 256),)),
        "edge_latents": scatter_about(keys[1], (EDGES, D), 1.0, 6.0, ((0, 256),)),
        "senders": draw_senders(jax.random.fold_in(keys[14], 71), 0),
        "receiver_tile": with_ends(jax.random.randint(keys[3], (ETILE * DEVICES,), 0, NTILE), jax.random.fold_in(keys[3], 1), 0, NTILE - 1).astype(jnp.int32),
        "receiver_row": with_ends(jax.random.randint(keys[4], (EDGES,), 0, TILE), jax.random.fold_in(keys[4], 1), 0, TILE - 1).astype(jnp.int32),
        "edge_mask": draw_edge_mask(jax.random.fold_in(keys[14], 71), 0),
        "send_map": draw_send_map(jax.random.fold_in(keys[14], 71), 0),
        "w_edge": scatter_about(keys[7], (D, D), (3 * D) ** -0.5, 0.15625),
        "w_send": scatter_about(keys[8], (D, D), (3 * D) ** -0.5, 0.15625),
        "w_recv": scatter_about(keys[9], (D, D), (3 * D) ** -0.5, 0.15625),
        "w_edge_out": scatter_about(keys[10], (D, D), D ** -0.5, 0.25),
        "w_node": scatter_about(keys[11], (D, D), (2 * D) ** -0.5, 0.1875),
        "w_node_agg": scatter_about(keys[12], (D, D), (2 * D) ** -0.5, 0.1875),
        "w_node_out": scatter_about(keys[13], (D, D), D ** -0.5, 0.25),
    }


def layer_norm(values):
    centred = values - lax.optimization_barrier(jnp.mean(values, axis=-1, keepdims=True))
    return centred * lax.rsqrt(lax.optimization_barrier(jnp.mean(centred * centred, axis=-1, keepdims=True)) + 1e-05)

def reference(node_latents, edge_latents, senders, receiver_tile, receiver_row, edge_mask, send_map, w_edge, w_send, w_recv, w_edge_out, w_node, w_node_agg, w_node_out):
    device_count = N_REGION * N_GROUP
    node_rows = NTILE * TILE
    edge_rows = ETILE * TILE
    feature_width = node_latents.shape[1]
    sender_proj = jnp.dot(node_latents, w_send, preferred_element_type=jnp.float32).astype(jnp.bfloat16)
    receiver_proj = jnp.dot(node_latents, w_recv, preferred_element_type=jnp.float32).astype(jnp.bfloat16)
    proj_tiles = sender_proj.reshape(device_count, NTILE, TILE, feature_width)
    recv_all = receiver_proj.reshape(device_count, node_rows, feature_width)
    nodes_all = node_latents.reshape(device_count, node_rows, feature_width)
    edges_all = edge_latents.reshape(device_count, edge_rows, feature_width)
    senders_all = senders.reshape(device_count, edge_rows)
    receivers_all = (receiver_tile.reshape(device_count, ETILE, 1) * TILE + receiver_row.reshape(device_count, ETILE, TILE)).reshape(device_count, edge_rows)
    mask_all = edge_mask.reshape(device_count, edge_rows)

    def one_device(index):
        region_id = index // N_GROUP
        group_id = index % N_GROUP
        lower_id = (region_id - 1) % N_REGION * N_GROUP + group_id
        upper_id = (region_id + 1) % N_REGION * N_GROUP + group_id
        from_lower = proj_tiles[lower_id][send_map[lower_id, 1]].reshape(-1, feature_width)
        from_upper = proj_tiles[upper_id][send_map[upper_id, 0]].reshape(-1, feature_width)
        members = region_id * N_GROUP + jnp.arange(N_GROUP, dtype=jnp.int32)
        coarse_panel = proj_tiles[members][:, :CT].reshape(-1, feature_width)
        sender_table = jnp.concatenate([proj_tiles[index].reshape(-1, feature_width), from_lower, from_upper, coarse_panel], axis=0)
        receivers = receivers_all[index]
        edge_here = edges_all[index]
        pre_act = jnp.dot(edge_here, w_edge, preferred_element_type=jnp.float32)
        pre_act = pre_act + sender_table[senders_all[index]].astype(jnp.float32) + recv_all[index][receivers].astype(jnp.float32)
        hidden = jax.nn.silu(pre_act).astype(jnp.bfloat16)
        edge_out = jnp.dot(hidden, w_edge_out, preferred_element_type=jnp.float32)
        message = layer_norm(edge_out) * mask_all[index].astype(jnp.float32)[:, None]
        new_edges = (edge_here.astype(jnp.float32) + message).astype(jnp.bfloat16)
        message_low = message.astype(jnp.bfloat16).astype(jnp.float32)
        aggregated = jax.ops.segment_sum(message_low, receivers, num_segments=node_rows).astype(jnp.bfloat16)
        node_here = nodes_all[index]
        node_pre = jnp.dot(node_here, w_node, preferred_element_type=jnp.float32) + jnp.dot(aggregated, w_node_agg, preferred_element_type=jnp.float32)
        node_hidden = jax.nn.silu(node_pre).astype(jnp.bfloat16)
        node_out = jnp.dot(node_hidden, w_node_out, preferred_element_type=jnp.float32)
        new_nodes = (node_here.astype(jnp.float32) + layer_norm(node_out)).astype(jnp.bfloat16)
        return (new_nodes, new_edges)
    new_nodes, new_edges = lax.map(one_device, jnp.arange(device_count, dtype=jnp.int32))
    return (new_nodes.reshape(-1, feature_width), new_edges.reshape(-1, feature_width))
```

```python
import functools

import jax
import jax.numpy as jnp
from jax import lax
from jax.experimental import pallas as pl
from jax.experimental.pallas import tpu as pltpu
from jax.sharding import PartitionSpec as P

TILE = 128
D = 512
NTILE = 8
ETILE = 32
NODES = NTILE * TILE
EDGES = ETILE * TILE
REMOTE = 1536
TABLE = NODES + REMOTE
LANES = 128
PIECES = D // LANES
BLOCK = 512
BF = jnp.bfloat16
F32 = jnp.float32

ANY = pl.BlockSpec(memory_space=pl.ANY)
SMEM = pl.BlockSpec(memory_space=pltpu.SMEM)
VMEM = pl.BlockSpec(memory_space=pltpu.VMEM)


def in_vmem(x):
    return pltpu.with_memory_space_constraint(x, pltpu.VMEM)


def in_hbm(x):
    return pltpu.with_memory_space_constraint(x, pltpu.HBM)


def whole(shape):
    return pl.BlockSpec(shape, lambda i: (0,) * len(shape))


def dot(a, b):
    return jnp.dot(a, b, preferred_element_type=F32)


def silu(x):
    return x * (0.5 + 0.5 * jnp.tanh(0.5 * x))


def normed(v):
    centred = v - jnp.sum(v, axis=-1, keepdims=True) * (1.0 / D)
    var = jnp.sum(centred * centred, axis=-1, keepdims=True) * (1.0 / D)
    return centred, lax.rsqrt(var + 1e-05)


def put_rows(table, first, value):
    for c in range(PIECES):
        table[pl.ds(first * PIECES + c, value.shape[0], stride=PIECES), :] = value[
            :, c * LANES : (c + 1) * LANES
        ]


def get_rows(table, first, rows):
    return jnp.concatenate(
        [table[pl.ds(first * PIECES + c, rows, stride=PIECES), :] for c in range(PIECES)], axis=-1
    )


def one_hot(row_of_edge):
    rows = lax.broadcasted_iota(jnp.int32, (TILE, TILE), 0)
    return (rows == row_of_edge).astype(BF)


def pick_kernel(send_map, nodes, coarse, lower, upper, map_s, map_sem, sems):
    me = lax.axis_index("region") * lax.axis_size("group") + lax.axis_index("group")
    get_map = pltpu.make_async_copy(send_map, map_s, map_sem)
    get_map.start()
    copies = [pltpu.make_async_copy(nodes.at[pl.ds(0, TILE)], coarse, sems.at[0])]
    copies[0].start()
    get_map.wait()
    for side, out in ((0, lower), (1, upper)):
        for j in range(2):
            tile = map_s[side, j, me]
            copies.append(
                pltpu.make_async_copy(
                    nodes.at[pl.ds(pl.multiple_of(tile * TILE, TILE), TILE)],
                    out.at[pl.ds(j * TILE, TILE)],
                    sems.at[1 + side * 2 + j],
                )
            )
            copies[-1].start()
    for copy in copies:
        copy.wait()


def pick(node_latents, send_map):
    by_side = jnp.transpose(send_map, (1, 2, 0))
    return pl.pallas_call(
        pick_kernel,
        out_shape=[jax.ShapeDtypeStruct((rows, D), BF) for rows in (TILE, 2 * TILE, 2 * TILE)],
        in_specs=[ANY, ANY],
        out_specs=[VMEM] * 3,
        scratch_shapes=[
            pltpu.SMEM(by_side.shape, jnp.int32),
            pltpu.SemaphoreType.DMA,
            pltpu.SemaphoreType.DMA((5,)),
        ],
        compiler_params=pltpu.CompilerParams(vmem_limit_bytes=16 << 20),
        name="pick",
    )(in_hbm(by_side), in_hbm(node_latents))


def early_kernel(
    recv_tile, recv_row, nodes_h, edges_b, we_h, ws_h, wr_h, wn_h, weo_h, wna_h, wno_h,
    pre, edges, table, node_pre, nodes, ws, weo, wna, wno,
    we, wr, wn, recv_proj, sems,
):
    i = pl.program_id(0)
    pairs = [
        (nodes_h, nodes), (ws_h, ws), (wr_h, wr), (wn_h, wn), (we_h, we),
        (weo_h, weo), (wna_h, wna), (wno_h, wno),
    ]
    copies = [pltpu.make_async_copy(a, b, sems.at[j]) for j, (a, b) in enumerate(pairs)]

    @pl.when(i == 0)
    def _():
        for copy in copies:
            copy.start()
        for copy in copies:
            copy.wait()
        for k in range(NODES // BLOCK):
            part = slice(BLOCK * k, BLOCK * (k + 1))
            x = nodes[part]
            put_rows(table, BLOCK * k, dot(x, ws[...]).astype(BF).astype(F32))
            recv_proj[part] = dot(x, wr[...]).astype(BF)
            node_pre[part] = dot(x, wn[...])

    x = edges_b[...]
    here = pl.ds(pl.multiple_of(i * BLOCK, BLOCK), BLOCK)
    edges[here, :] = x
    own = dot(x, we[...])
    received = []
    for t in range(BLOCK // TILE):
        tile = recv_tile[i * (BLOCK // TILE) + t]
        hot = one_hot(recv_row[pl.ds(i * (BLOCK // TILE) + t, 1), :])
        received.append(
            lax.dot_general(
                hot,
                recv_proj[pl.ds(pl.multiple_of(tile * TILE, TILE), TILE), :],
                (((0,), (0,)), ((), ())),
                preferred_element_type=F32,
            )
        )
    pre[here, :] = own + jnp.concatenate(received)


def early(recv_tile, recv_row, nodes, edges, w_edge, w_send, w_recv, w_node, w_edge_out, w_node_agg, w_node_out):
    weight = pltpu.VMEM((D, D), BF)
    return pl.pallas_call(
        early_kernel,
        grid=(EDGES // BLOCK,),
        out_shape=[
            pltpu.VMEM((EDGES, D), F32),
            pltpu.VMEM((EDGES, D), BF),
            pltpu.VMEM((TABLE * PIECES, LANES), F32),
            pltpu.VMEM((NODES, D), F32),
            pltpu.VMEM((NODES, D), BF),
            weight, weight, weight, weight,
        ],
        in_specs=[SMEM, whole((ETILE, TILE)), ANY, pl.BlockSpec((BLOCK, D), lambda i: (i, 0))] + [ANY] * 7,
        out_specs=[VMEM] * 9,
        scratch_shapes=[weight, weight, weight, pltpu.VMEM((NODES, D), BF), pltpu.SemaphoreType.DMA((8,))],
        compiler_params=pltpu.CompilerParams(vmem_limit_bytes=20 << 20),
        cost_estimate=pl.CostEstimate(flops=8 << 30, bytes_accessed=24 << 20, transcendentals=0),
        name="early",
    )(
        recv_tile, recv_row, in_hbm(nodes), in_hbm(edges),
        *[in_hbm(w) for w in (w_edge, w_send, w_recv, w_node, w_edge_out, w_node_agg, w_node_out)],
    )


def late_kernel(
    senders, recv_tile, recv_row, mask,
    low, up, p_z, p_x1, p_x3, p_x2, p_z1, p_z3, p_z2,
    pre, edges, table_in, node_pre, nodes, ws, weo, wna, wno,
    out_nodes, out_edges, table,
    remote, picked, total, live, sems,
):
    i = pl.program_id(0)
    tiles = BLOCK // TILE

    @pl.when(i == 0)
    def _():
        me = lax.axis_index("group")
        panel = [
            (p_z, me ^ 1), (p_x1, (me + 6) % 8), (p_x3, (me + 2) % 8), (p_x2, (me + 4) % 8),
            (p_z1, ((me + 6) % 8) ^ 1), (p_z3, ((me + 2) % 8) ^ 1), (p_z2, ((me + 4) % 8) ^ 1),
        ]
        copies = [
            pltpu.make_async_copy(low, remote.at[pl.ds(0, 2 * TILE)], sems.at[0]),
            pltpu.make_async_copy(up, remote.at[pl.ds(2 * TILE, 2 * TILE)], sems.at[1]),
        ]
        for j, (piece, member) in enumerate(panel):
            at = pl.multiple_of(4 * TILE + member * TILE, TILE)
            copies.append(pltpu.make_async_copy(piece, remote.at[pl.ds(at, TILE)], sems.at[2 + j]))
        for copy in copies:
            copy.start()
        remote[pl.ds(pl.multiple_of(4 * TILE + me * TILE, TILE), TILE), :] = nodes[0:TILE, :]
        total[...] = jnp.zeros_like(total)
        live[0] = jnp.sum(mask[...])
        for copy in copies:
            copy.wait()
        for k in range(REMOTE // BLOCK):
            proj = dot(remote[BLOCK * k : BLOCK * (k + 1)], ws[...])
            put_rows(table, NODES + BLOCK * k, proj.astype(BF).astype(F32))

    first = pl.multiple_of(i * BLOCK, BLOCK)
    for e in range(BLOCK):
        row = senders[first + e]
        picked[e * PIECES : (e + 1) * PIECES, :] = table[
            pl.ds(pl.multiple_of(row * PIECES, PIECES), PIECES), :
        ]
    hidden = silu(pre[pl.ds(first, BLOCK), :] + get_rows(picked, 0, BLOCK)).astype(BF)
    centred, scale = normed(dot(hidden, weo[...]))
    slot = lax.broadcasted_iota(jnp.int32, (BLOCK, 1), 0) + first
    message = centred * jnp.where(slot < live[0], scale, 0.0)
    out_edges[...] = (edges[pl.ds(first, BLOCK), :].astype(F32) + message).astype(BF)
    rounded = message.astype(BF)
    for t in range(tiles):
        hot = one_hot(recv_row[pl.ds(i * tiles + t, 1), :])
        total[recv_tile[i * tiles + t]] += dot(hot, rounded[t * TILE : (t + 1) * TILE])

    @pl.when(i == EDGES // BLOCK - 1)
    def _():
        per = BLOCK // TILE
        for k in range(NODES // BLOCK):
            part = slice(BLOCK * k, BLOCK * (k + 1))
            summed = total[per * k : per * (k + 1)].reshape(BLOCK, D).astype(BF)
            hidden_n = silu(node_pre[part] + dot(summed, wna[...])).astype(BF)
            centred_n, scale_n = normed(dot(hidden_n, wno[...]))
            out_nodes[part, :] = (nodes[part].astype(F32) + centred_n * scale_n).astype(BF)


def late(senders, recv_tile, recv_row, mask, pieces, kept):
    return pl.pallas_call(
        late_kernel,
        grid=(EDGES // BLOCK,),
        out_shape=[
            jax.ShapeDtypeStruct((NODES, D), BF),
            jax.ShapeDtypeStruct((EDGES, D), BF),
            pltpu.VMEM((TABLE * PIECES, LANES), F32),
        ],
        in_specs=[SMEM, SMEM, whole((ETILE, TILE)), whole((ETILE, TILE))] + [ANY] * 9 + [VMEM] * 9,
        out_specs=[whole((NODES, D)), pl.BlockSpec((BLOCK, D), lambda i: (i, 0)), VMEM],
        input_output_aliases={15: 2},
        scratch_shapes=[
            pltpu.VMEM((REMOTE, D), BF),
            pltpu.VMEM((BLOCK * PIECES, LANES), F32),
            pltpu.VMEM((NTILE, TILE, D), F32),
            pltpu.SMEM((1,), jnp.int32),
            pltpu.SemaphoreType.DMA((9,)),
        ],
        compiler_params=pltpu.CompilerParams(vmem_limit_bytes=28 << 20),
        cost_estimate=pl.CostEstimate(flops=8 << 30, bytes_accessed=16 << 20, transcendentals=0),
        name="late",
    )(senders, recv_tile, recv_row, mask, *[in_hbm(p) for p in pieces], *[in_vmem(k) for k in kept])[:2]


def moved(x, axis, by):
    size = lax.axis_size(axis)
    return lax.ppermute(x, axis, [(i, (i + by) % size) for i in range(size)])


def per_device(
    node_latents, edge_latents, senders, receiver_tile, receiver_row, edge_mask, send_map,
    w_edge, w_send, w_recv, w_edge_out, w_node, w_node_agg, w_node_out,
):
    coarse, to_lower, to_upper = pick(node_latents, send_map)
    p_z = lax.ppermute(coarse, "group", [(i, i ^ 1) for i in range(8)])
    p_x = [moved(coarse, "group", by) for by in (2, 6, 4)]
    from_lower = moved(to_upper, "region", 1)
    from_upper = moved(to_lower, "region", -1)
    p_xz = [moved(p_z, "group", by) for by in (2, 6, 4)]
    recv_row = receiver_row.reshape(ETILE, TILE)
    kept = early(
        receiver_tile, recv_row, node_latents, edge_latents,
        w_edge, w_send, w_recv, w_node, w_edge_out, w_node_agg, w_node_out,
    )
    return late(
        senders, receiver_tile, recv_row, edge_mask.reshape(ETILE, TILE),
        [from_lower, from_upper, p_z] + p_x + p_xz, kept,
    )


def solution(mesh):
    by_device = P(("region", "group"))
    rows = P(("region", "group"), None)
    return jax.shard_map(
        per_device,
        mesh=mesh,
        in_specs=(rows, rows) + (by_device,) * 4 + (P(),) * 8,
        out_specs=(rows, rows),
        check_vma=False,
    )
```

```python
import functools

import jax
import jax.numpy as jnp
from jax import lax
from jax.experimental import pallas as pl
from jax.experimental.pallas import tpu as pltpu
from jax.sharding import PartitionSpec as P

TILE = 128
D = 512
NTILE = 8
ETILE = 32
NODES = NTILE * TILE
EDGES = ETILE * TILE
REMOTE = 1536
TABLE = NODES + REMOTE
LANES = 128
PIECES = D // LANES
BLOCK = 512
BF = jnp.bfloat16
F32 = jnp.float32

ANY = pl.BlockSpec(memory_space=pl.ANY)
SMEM = pl.BlockSpec(memory_space=pltpu.SMEM)
VMEM = pl.BlockSpec(memory_space=pltpu.VMEM)


def in_vmem(x):
    return pltpu.with_memory_space_constraint(x, pltpu.VMEM)


def in_hbm(x):
    return pltpu.with_memory_space_constraint(x, pltpu.HBM)


def whole(shape):
    return pl.BlockSpec(shape, lambda i: (0,) * len(shape))


def dot(a, b):
    return jnp.dot(a, b, preferred_element_type=F32)


def normed(v):
    centred = v - jnp.sum(v, axis=-1, keepdims=True) * (1.0 / D)
    var = jnp.sum(centred * centred, axis=-1, keepdims=True) * (1.0 / D)
    return centred, lax.rsqrt(var + 1e-05)


def put_rows(table, first, value):
    for c in range(PIECES):
        table[pl.ds(first * PIECES + c, value.shape[0], stride=PIECES), :] = value[
            :, c * LANES : (c + 1) * LANES
        ]


def get_rows(table, first, rows):
    return jnp.concatenate(
        [table[pl.ds(first * PIECES + c, rows, stride=PIECES), :] for c in range(PIECES)], axis=-1
    )


def one_hot(row_of_edge):
    rows = lax.broadcasted_iota(jnp.int32, (TILE, TILE), 0)
    return (rows == row_of_edge).astype(BF)


def first_kernel(nodes, coarse):
    coarse[...] = nodes[...]


def first_tile(node_latents):
    block = pl.BlockSpec((TILE, D), lambda i: (0, 0))
    return pl.pallas_call(
        first_kernel,
        grid=(1,),
        out_shape=jax.ShapeDtypeStruct((TILE, D), BF),
        in_specs=[block],
        out_specs=block,
        compiler_params=pltpu.CompilerParams(vmem_limit_bytes=4 << 20),
        name="first_tile",
    )(in_hbm(node_latents))


def project_kernel(
    send_map, nodes_h, ws_h, wr_h, wn_h, we_h, weo_h, wna_h, wno_h,
    coarse, lower, upper, table, node_pre, nodes, recv_proj, ws, we, weo, wna, wno,
    wr, wn, map_s, map_sem, sems, out_sems,
):
    me = lax.axis_index("region") * lax.axis_size("group") + lax.axis_index("group")
    get_map = pltpu.make_async_copy(send_map, map_s, map_sem)
    get_map.start()
    pairs = [
        (nodes_h, nodes), (ws_h, ws), (wr_h, wr), (wn_h, wn), (we_h, we),
        (weo_h, weo), (wna_h, wna), (wno_h, wno),
    ]
    copies = [pltpu.make_async_copy(a, b, sems.at[j]) for j, (a, b) in enumerate(pairs)]
    for copy in copies:
        copy.start()
    get_map.wait()
    copies[0].wait()
    sent = [pltpu.make_async_copy(nodes.at[pl.ds(0, TILE)], coarse, out_sems.at[0])]
    for side, out in ((0, lower), (1, upper)):
        for j in range(2):
            tile = map_s[side, j, me]
            sent.append(
                pltpu.make_async_copy(
                    nodes.at[pl.ds(pl.multiple_of(tile * TILE, TILE), TILE)],
                    out.at[pl.ds(j * TILE, TILE)],
                    out_sems.at[1 + side * 2 + j],
                )
            )
    for copy in sent:
        copy.start()
    for copy in copies[1:4]:
        copy.wait()
    for k in range(NODES // BLOCK):
        part = slice(BLOCK * k, BLOCK * (k + 1))
        x = nodes[part]
        put_rows(table, BLOCK * k, 0.5 * dot(x, ws[...]).astype(BF).astype(F32))
        recv_proj[part] = dot(x, wr[...]).astype(BF)
        node_pre[part] = dot(x, wn[...])
    for copy in copies[4:] + sent:
        copy.wait()


def project(send_map, nodes, w_send, w_recv, w_node, w_edge, w_edge_out, w_node_agg, w_node_out):
    weight = pltpu.VMEM((D, D), BF)
    by_side = jnp.transpose(send_map, (1, 2, 0))
    return pl.pallas_call(
        project_kernel,
        out_shape=[
            jax.ShapeDtypeStruct((TILE, D), BF),
            jax.ShapeDtypeStruct((2 * TILE, D), BF),
            jax.ShapeDtypeStruct((2 * TILE, D), BF),
            pltpu.VMEM((NODES * PIECES, LANES), F32),
            pltpu.VMEM((NODES, D), F32),
            pltpu.VMEM((NODES, D), BF),
            pltpu.VMEM((NODES, D), BF),
            weight, weight, weight, weight, weight,
        ],
        in_specs=[ANY] * 9,
        out_specs=[ANY] * 3 + [VMEM] * 9,
        scratch_shapes=[
            weight,
            weight,
            pltpu.SMEM(by_side.shape, jnp.int32),
            pltpu.SemaphoreType.DMA,
            pltpu.SemaphoreType.DMA((8,)),
            pltpu.SemaphoreType.DMA((5,)),
        ],
        compiler_params=pltpu.CompilerParams(vmem_limit_bytes=16 << 20),
        cost_estimate=pl.CostEstimate(flops=4 << 30, bytes_accessed=12 << 20, transcendentals=0),
        name="project",
    )(*[in_hbm(v) for v in (by_side, nodes, w_send, w_recv, w_node, w_edge, w_edge_out, w_node_agg, w_node_out)])


def early_kernel(recv_tile, recv_row, senders, edges_h, recv_proj, we, pre, edges, table_at, sems):
    blocks = EDGES // BLOCK
    tiles = BLOCK // TILE

    def get(b):
        here = pl.ds(pl.multiple_of(b * BLOCK, BLOCK), BLOCK)
        return pltpu.make_async_copy(edges_h.at[here], edges.at[here], sems.at[b])

    for b in range(blocks):
        get(b).start()
    table_at[...] = senders[...] * PIECES

    def body(b, _):
        get(b).wait()
        here = pl.ds(pl.multiple_of(b * BLOCK, BLOCK), BLOCK)
        own = dot(edges[here, :], we[...])
        received = []
        for t in range(tiles):
            tile = recv_tile[b * tiles + t]
            hot = one_hot(recv_row[pl.ds(b * tiles + t, 1), :])
            received.append(
                lax.dot_general(
                    hot,
                    recv_proj[pl.ds(pl.multiple_of(tile * TILE, TILE), TILE), :],
                    (((0,), (0,)), ((), ())),
                    preferred_element_type=F32,
                )
            )
        pre[here, :] = 0.5 * (own + jnp.concatenate(received))
        return 0

    lax.fori_loop(0, blocks, body, 0)


def early(recv_tile, recv_row, senders, edges, recv_proj, we):
    return pl.pallas_call(
        early_kernel,
        out_shape=[
            pltpu.VMEM((EDGES, D), F32),
            pltpu.VMEM((EDGES, D), BF),
            jax.ShapeDtypeStruct((ETILE, TILE), jnp.int32),
        ],
        in_specs=[SMEM, VMEM, VMEM, ANY, VMEM, VMEM],
        out_specs=[VMEM] * 3,
        scratch_shapes=[pltpu.SemaphoreType.DMA((EDGES // BLOCK,))],
        compiler_params=pltpu.CompilerParams(vmem_limit_bytes=16 << 20),
        cost_estimate=pl.CostEstimate(flops=8 << 30, bytes_accessed=24 << 20, transcendentals=0),
        name="early",
    )(recv_tile, recv_row, senders, in_hbm(edges), in_vmem(recv_proj), in_vmem(we))


def late_kernel(
    table_at, recv_tile, recv_row, mask,
    low, up, p_z, p_x1, p_x3, p_x2,
    pre, edges_in, own_table, node_pre, nodes, ws, weo, wna, wno,
    out_nodes, out_edges, edges,
    table, remote, picked, total, new_nodes, own_sem, sems, out_sems,
):
    tiles = BLOCK // TILE
    blocks = EDGES // BLOCK
    me = lax.axis_index("group")
    panel = [(p_z, me ^ 1)]
    for pair, member in ((p_x1, (me + 6) % 8), (p_x3, (me + 2) % 8), (p_x2, (me + 4) % 8)):
        panel.append((pair.at[pl.ds(0, TILE)], member))
        panel.append((pair.at[pl.ds(TILE, TILE)], member ^ 1))
    copies = [
        pltpu.make_async_copy(low, remote.at[pl.ds(0, 2 * TILE)], sems.at[0]),
        pltpu.make_async_copy(up, remote.at[pl.ds(2 * TILE, 2 * TILE)], sems.at[1]),
    ]
    for j, (piece, member) in enumerate(panel):
        at = pl.multiple_of(4 * TILE + member * TILE, TILE)
        copies.append(pltpu.make_async_copy(piece, remote.at[pl.ds(at, TILE)], sems.at[2 + j]))
    for copy in copies:
        copy.start()
    own = pltpu.make_async_copy(own_table, table.at[pl.ds(0, NODES * PIECES)], own_sem)
    own.start()

    remote[pl.ds(pl.multiple_of(4 * TILE + me * TILE, TILE), TILE), :] = nodes[0:TILE, :]
    total[...] = jnp.zeros_like(total)
    live = jnp.sum(mask[...])
    for copy in copies:
        copy.wait()
    for k in range(REMOTE // BLOCK):
        proj = dot(remote[BLOCK * k : BLOCK * (k + 1)], ws[...])
        put_rows(table, NODES + BLOCK * k, 0.5 * proj.astype(BF).astype(F32))
    own.wait()

    def put_edges(b):
        here = pl.ds(pl.multiple_of(b * BLOCK, BLOCK), BLOCK)
        return pltpu.make_async_copy(edges.at[here], out_edges.at[here], out_sems.at[b])

    def body(b, _):
        first = pl.multiple_of(b * BLOCK, BLOCK)
        here = pl.ds(first, BLOCK)
        for e in range(BLOCK):
            picked[e * PIECES : (e + 1) * PIECES, :] = table[
                pl.ds(pl.multiple_of(table_at[first + e], PIECES), PIECES), :
            ]
        half = pre[here, :] + get_rows(picked, 0, BLOCK)
        hidden = (half + half * jnp.tanh(half)).astype(BF)
        centred, scale = normed(dot(hidden, weo[...]))
        slot = lax.broadcasted_iota(jnp.int32, (BLOCK, 1), 0) + first
        message = centred * jnp.where(slot < live, scale, 0.0)
        edges[here, :] = (edges[here, :].astype(F32) + message).astype(BF)
        put_edges(b).start()
        rounded = message.astype(BF)
        for t in range(tiles):
            hot = one_hot(recv_row[pl.ds(b * tiles + t, 1), :])
            total[recv_tile[b * tiles + t]] += dot(hot, rounded[t * TILE : (t + 1) * TILE])
        return 0

    lax.fori_loop(0, blocks, body, 0)
    sent = []
    for k in range(NODES // BLOCK):
        part = slice(BLOCK * k, BLOCK * (k + 1))
        summed = total[tiles * k : tiles * (k + 1)].reshape(BLOCK, D).astype(BF)
        half_n = 0.5 * (node_pre[part] + dot(summed, wna[...]))
        hidden_n = (half_n + half_n * jnp.tanh(half_n)).astype(BF)
        centred_n, scale_n = normed(dot(hidden_n, wno[...]))
        new_nodes[part] = (nodes[part].astype(F32) + centred_n * scale_n).astype(BF)
        for t in range(tiles):
            here = pl.ds(BLOCK * k + TILE * t, TILE)
            sent.append(
                pltpu.make_async_copy(
                    new_nodes.at[here], out_nodes.at[here], out_sems.at[blocks + tiles * k + t]
                )
            )
            sent[-1].start()
    for copy in sent:
        copy.wait()
    for b in range(blocks):
        put_edges(b).wait()


def late(table_at, recv_tile, recv_row, mask, pieces, kept):
    blocks = EDGES // BLOCK
    return pl.pallas_call(
        late_kernel,
        out_shape=[
            jax.ShapeDtypeStruct((NODES, D), BF),
            jax.ShapeDtypeStruct((EDGES, D), BF),
            pltpu.VMEM((EDGES, D), BF),
        ],
        in_specs=[SMEM, SMEM, VMEM, VMEM] + [ANY] * 6 + [VMEM] * 9,
        out_specs=[ANY, ANY, VMEM],
        input_output_aliases={11: 2},
        scratch_shapes=[
            pltpu.VMEM((TABLE * PIECES, LANES), F32),
            pltpu.VMEM((REMOTE, D), BF),
            pltpu.VMEM((BLOCK * PIECES, LANES), F32),
            pltpu.VMEM((NTILE, TILE, D), F32),
            pltpu.VMEM((NODES, D), BF),
            pltpu.SemaphoreType.DMA,
            pltpu.SemaphoreType.DMA((9,)),
            pltpu.SemaphoreType.DMA((blocks + NTILE,)),
        ],
        compiler_params=pltpu.CompilerParams(vmem_limit_bytes=28 << 20),
        cost_estimate=pl.CostEstimate(flops=8 << 30, bytes_accessed=16 << 20, transcendentals=0),
        name="late",
    )(table_at, recv_tile, recv_row, mask, *pieces, *[in_vmem(k) for k in kept])[:2]


def joined_kernel(a, b, out, sems):
    copies = [
        pltpu.make_async_copy(a, out.at[pl.ds(0, TILE)], sems.at[0]),
        pltpu.make_async_copy(b, out.at[pl.ds(TILE, TILE)], sems.at[1]),
    ]
    for copy in copies:
        copy.start()
    for copy in copies:
        copy.wait()


def joined(a, b):
    return pl.pallas_call(
        joined_kernel,
        out_shape=jax.ShapeDtypeStruct((2 * TILE, D), BF),
        in_specs=[ANY, ANY],
        out_specs=VMEM,
        scratch_shapes=[pltpu.SemaphoreType.DMA((2,))],
        compiler_params=pltpu.CompilerParams(vmem_limit_bytes=4 << 20),
        name="joined",
    )(a, b)


def moved(x, axis, by):
    size = lax.axis_size(axis)
    return lax.ppermute(x, axis, [(i, (i + by) % size) for i in range(size)])


def per_device(
    node_latents, edge_latents, senders, receiver_tile, receiver_row, edge_mask, send_map,
    w_edge, w_send, w_recv, w_edge_out, w_node, w_node_agg, w_node_out,
):
    p_z = lax.ppermute(first_tile(node_latents), "group", [(i, i ^ 1) for i in range(8)])
    coarse, to_lower, to_upper, table, node_pre, nodes, recv_proj, ws, we, weo, wna, wno = project(
        send_map, node_latents, w_send, w_recv, w_node, w_edge, w_edge_out, w_node_agg, w_node_out
    )
    both = joined(coarse, p_z)
    p_x = [moved(both, "group", by) for by in (2, 6, 4)]
    from_lower = moved(to_upper, "region", 1)
    from_upper = moved(to_lower, "region", -1)
    recv_row = receiver_row.reshape(ETILE, TILE)
    pre, edges, table_at = early(
        receiver_tile, recv_row, senders.reshape(ETILE, TILE), edge_latents, recv_proj, we
    )
    return late(
        table_at.reshape(EDGES), receiver_tile, recv_row, edge_mask.reshape(ETILE, TILE),
        [from_lower, from_upper, p_z] + p_x,
        [pre, edges, table, node_pre, nodes, ws, weo, wna, wno],
    )


def solution(mesh):
    by_device = P(("region", "group"))
    rows = P(("region", "group"), None)
    return jax.shard_map(
        per_device,
        mesh=mesh,
        in_specs=(rows, rows) + (by_device,) * 4 + (P(),) * 8,
        out_specs=(rows, rows),
        check_vma=False,
    )
```

```python
import functools

import jax
import jax.numpy as jnp
from jax import lax
from jax.experimental import pallas as pl
from jax.experimental.pallas import tpu as pltpu
from jax.sharding import PartitionSpec as P

TILE = 128
D = 512
NTILE = 8
ETILE = 32
NODES = NTILE * TILE
EDGES = ETILE * TILE
REMOTE = 1536
TABLE = NODES + REMOTE
LANES = 128
PIECES = D // LANES
BLOCK = 512
BF = jnp.bfloat16
F32 = jnp.float32

ANY = pl.BlockSpec(memory_space=pl.ANY)
SMEM = pl.BlockSpec(memory_space=pltpu.SMEM)
VMEM = pl.BlockSpec(memory_space=pltpu.VMEM)


def in_vmem(x):
    return pltpu.with_memory_space_constraint(x, pltpu.VMEM)


def in_hbm(x):
    return pltpu.with_memory_space_constraint(x, pltpu.HBM)


def whole(shape):
    return pl.BlockSpec(shape, lambda i: (0,) * len(shape))


def dot(a, b):
    return jnp.dot(a, b, preferred_element_type=F32)


def normed(v):
    centred = v - jnp.sum(v, axis=-1, keepdims=True) * (1.0 / D)
    var = jnp.sum(centred * centred, axis=-1, keepdims=True) * (1.0 / D)
    return centred, lax.rsqrt(var + 1e-05)


def put_rows(table, first, value):
    for c in range(PIECES):
        table[pl.ds(first * PIECES + c, value.shape[0], stride=PIECES), :] = value[
            :, c * LANES : (c + 1) * LANES
        ]


def get_rows(table, first, rows):
    return jnp.concatenate(
        [table[pl.ds(first * PIECES + c, rows, stride=PIECES), :] for c in range(PIECES)], axis=-1
    )


def one_hot(row_of_edge):
    rows = lax.broadcasted_iota(jnp.int32, (TILE, TILE), 0)
    return (rows == row_of_edge).astype(BF)


def first_kernel(nodes, coarse):
    coarse[...] = nodes[...]


def first_tile(node_latents):
    block = pl.BlockSpec((TILE, D), lambda i: (0, 0))
    return pl.pallas_call(
        first_kernel,
        grid=(1,),
        out_shape=jax.ShapeDtypeStruct((TILE, D), BF),
        in_specs=[block],
        out_specs=block,
        compiler_params=pltpu.CompilerParams(vmem_limit_bytes=4 << 20),
        name="first_tile",
    )(in_hbm(node_latents))


def project_kernel(
    send_map, nodes_h, ws_h, wr_h, wn_h, we_h, weo_h, wna_h, wno_h,
    coarse, inside, across, table, node_pre, nodes, recv_proj, ws, we, weo, wna, wno,
    wr, wn, map_s, map_sem, sems, out_sems,
):
    me = lax.axis_index("region") * lax.axis_size("group") + lax.axis_index("group")
    get_map = pltpu.make_async_copy(send_map, map_s, map_sem)
    get_map.start()
    pairs = [
        (nodes_h, nodes), (ws_h, ws), (wr_h, wr), (wn_h, wn), (we_h, we),
        (weo_h, weo), (wna_h, wna), (wno_h, wno),
    ]
    copies = [pltpu.make_async_copy(a, b, sems.at[j]) for j, (a, b) in enumerate(pairs)]
    for copy in copies:
        copy.start()
    get_map.wait()
    copies[0].wait()
    sent = [pltpu.make_async_copy(nodes.at[pl.ds(0, TILE)], coarse, out_sems.at[0])]
    odd = lax.rem(lax.axis_index("region"), 2)
    for k, (side, out) in enumerate(((1 - odd, inside), (odd, across))):
        for j in range(2):
            tile = map_s[side, j, me]
            sent.append(
                pltpu.make_async_copy(
                    nodes.at[pl.ds(pl.multiple_of(tile * TILE, TILE), TILE)],
                    out.at[pl.ds(j * TILE, TILE)],
                    out_sems.at[1 + k * 2 + j],
                )
            )
    for copy in sent:
        copy.start()
    for copy in copies[1:4]:
        copy.wait()
    for k in range(NODES // BLOCK):
        part = slice(BLOCK * k, BLOCK * (k + 1))
        x = nodes[part]
        put_rows(table, BLOCK * k, 0.5 * dot(x, ws[...]).astype(BF).astype(F32))
        recv_proj[part] = dot(x, wr[...]).astype(BF)
        node_pre[part] = dot(x, wn[...])
    for copy in copies[4:] + sent:
        copy.wait()


def project(send_map, nodes, w_send, w_recv, w_node, w_edge, w_edge_out, w_node_agg, w_node_out):
    weight = pltpu.VMEM((D, D), BF)
    by_side = jnp.transpose(send_map, (1, 2, 0))
    return pl.pallas_call(
        project_kernel,
        out_shape=[
            jax.ShapeDtypeStruct((TILE, D), BF),
            jax.ShapeDtypeStruct((2 * TILE, D), BF),
            jax.ShapeDtypeStruct((2 * TILE, D), BF),
            pltpu.VMEM((TABLE * PIECES, LANES), F32),
            pltpu.VMEM((NODES, D), F32),
            pltpu.VMEM((NODES, D), BF),
            pltpu.VMEM((NODES, D), BF),
            weight, weight, weight, weight, weight,
        ],
        in_specs=[ANY] * 9,
        out_specs=[ANY] * 3 + [VMEM] * 9,
        scratch_shapes=[
            weight,
            weight,
            pltpu.SMEM(by_side.shape, jnp.int32),
            pltpu.SemaphoreType.DMA,
            pltpu.SemaphoreType.DMA((8,)),
            pltpu.SemaphoreType.DMA((5,)),
        ],
        compiler_params=pltpu.CompilerParams(vmem_limit_bytes=16 << 20),
        cost_estimate=pl.CostEstimate(flops=4 << 30, bytes_accessed=12 << 20, transcendentals=0),
        name="project",
    )(*[in_hbm(v) for v in (by_side, nodes, w_send, w_recv, w_node, w_edge, w_edge_out, w_node_agg, w_node_out)])


def early_kernel(recv_tile, recv_row, senders, edges_h, recv_proj, we, pre, edges, table_at, total, sems):
    blocks = EDGES // BLOCK
    tiles = BLOCK // TILE

    def get(b):
        here = pl.ds(pl.multiple_of(b * BLOCK, BLOCK), BLOCK)
        return pltpu.make_async_copy(edges_h.at[here], edges.at[here], sems.at[b])

    for b in range(blocks):
        get(b).start()
    table_at[...] = senders[...] * PIECES
    total[...] = jnp.zeros_like(total)

    def body(b, _):
        get(b).wait()
        here = pl.ds(pl.multiple_of(b * BLOCK, BLOCK), BLOCK)
        own = dot(edges[here, :], we[...])
        received = []
        for t in range(tiles):
            tile = recv_tile[b * tiles + t]
            hot = one_hot(recv_row[pl.ds(b * tiles + t, 1), :])
            received.append(
                lax.dot_general(
                    hot,
                    recv_proj[pl.ds(pl.multiple_of(tile * TILE, TILE), TILE), :],
                    (((0,), (0,)), ((), ())),
                    preferred_element_type=F32,
                )
            )
        pre[here, :] = 0.5 * (own + jnp.concatenate(received))
        return 0

    lax.fori_loop(0, blocks, body, 0)


def early(recv_tile, recv_row, senders, edges, recv_proj, we):
    return pl.pallas_call(
        early_kernel,
        out_shape=[
            pltpu.VMEM((EDGES, D), F32),
            pltpu.VMEM((EDGES, D), BF),
            jax.ShapeDtypeStruct((ETILE, TILE), jnp.int32),
            pltpu.VMEM((NTILE, TILE, D), F32),
        ],
        in_specs=[SMEM, VMEM, VMEM, ANY, VMEM, VMEM],
        out_specs=[VMEM] * 4,
        scratch_shapes=[pltpu.SemaphoreType.DMA((EDGES // BLOCK,))],
        compiler_params=pltpu.CompilerParams(vmem_limit_bytes=16 << 20),
        cost_estimate=pl.CostEstimate(flops=8 << 30, bytes_accessed=24 << 20, transcendentals=0),
        name="early",
    )(recv_tile, recv_row, senders, in_hbm(edges), in_vmem(recv_proj), in_vmem(we))


def late_kernel(
    table_at, recv_tile, recv_row, mask,
    inside, across, p_z, p_xa, p_xb, p_x2,
    pre, edges_in, table_in, total_in, node_pre, nodes, ws, weo, wna, wno,
    out_nodes, out_edges, edges, table, total,
    remote, picked, new_nodes, sems, out_sems,
):
    tiles = BLOCK // TILE
    blocks = EDGES // BLOCK
    me = lax.axis_index("group")
    panel = [(p_z, me ^ 1)]
    side_x = jnp.where(lax.rem(lax.div(me, 2), 2) == 1, lax.rem(me + 2, 8), lax.rem(me + 6, 8))
    for pair, member in ((p_xa, me ^ 2), (p_xb, side_x), (p_x2, me ^ 4)):
        panel.append((pair.at[pl.ds(0, TILE)], member))
        panel.append((pair.at[pl.ds(TILE, TILE)], member ^ 1))
    odd = lax.rem(lax.axis_index("region"), 2)
    half_at = 2 * TILE
    copies = [
        pltpu.make_async_copy(inside, remote.at[pl.ds(pl.multiple_of((1 - odd) * half_at, half_at), half_at)], sems.at[0]),
        pltpu.make_async_copy(across, remote.at[pl.ds(pl.multiple_of(odd * half_at, half_at), half_at)], sems.at[1]),
    ]
    for j, (piece, member) in enumerate(panel):
        at = pl.multiple_of(4 * TILE + member * TILE, TILE)
        copies.append(pltpu.make_async_copy(piece, remote.at[pl.ds(at, TILE)], sems.at[2 + j]))
    for copy in copies:
        copy.start()

    remote[pl.ds(pl.multiple_of(4 * TILE + me * TILE, TILE), TILE), :] = nodes[0:TILE, :]
    live = jnp.sum(mask[...])
    for copy in copies:
        copy.wait()
    for k in range(REMOTE // BLOCK):
        proj = dot(remote[BLOCK * k : BLOCK * (k + 1)], ws[...])
        put_rows(table, NODES + BLOCK * k, 0.5 * proj.astype(BF).astype(F32))

    def put_edges(b):
        here = pl.ds(pl.multiple_of(b * BLOCK, BLOCK), BLOCK)
        return pltpu.make_async_copy(edges.at[here], out_edges.at[here], out_sems.at[b])

    def take(b, slot, start, stop):
        first = pl.multiple_of(b * BLOCK, BLOCK)
        for e in range(start, stop):
            to = (slot * BLOCK + e) * PIECES
            picked[to : to + PIECES, :] = table[pl.ds(pl.multiple_of(table_at[first + e], PIECES), PIECES), :]

    def edge_block(b, slot, b_next):
        first = pl.multiple_of(b * BLOCK, BLOCK)
        here = pl.ds(first, BLOCK)
        half = pre[here, :] + get_rows(picked, slot * BLOCK, BLOCK)
        hidden = (half + half * jnp.tanh(half)).astype(BF)
        out = dot(hidden, weo[...])
        parts = []
        for p in range(0, BLOCK, 32):
            take(b_next, 1 - slot, p, p + 32)
            centred, scale = normed(out[p : p + 32])
            slots = lax.broadcasted_iota(jnp.int32, (32, 1), 0) + (first + p)
            message = centred * jnp.where(slots < live, scale, 0.0)
            there = pl.ds(pl.multiple_of(first + p, 32), 32)
            edges[there, :] = (edges[there, :].astype(F32) + message).astype(BF)
            parts.append(message.astype(BF))
        put_edges(b).start()
        rounded = jnp.concatenate(parts)
        for t in range(tiles):
            hot = one_hot(recv_row[pl.ds(b * tiles + t, 1), :])
            total[recv_tile[b * tiles + t]] += dot(hot, rounded[t * TILE : (t + 1) * TILE])

    take(0, 0, 0, BLOCK)

    def body(j, _):
        edge_block(2 * j, 0, 2 * j + 1)
        edge_block(2 * j + 1, 1, jnp.minimum(2 * j + 2, blocks - 1))
        return 0

    lax.fori_loop(0, blocks // 2, body, 0)
    sent = []
    for k in range(NODES // BLOCK):
        part = slice(BLOCK * k, BLOCK * (k + 1))
        summed = total[tiles * k : tiles * (k + 1)].reshape(BLOCK, D).astype(BF)
        half_n = 0.5 * (node_pre[part] + dot(summed, wna[...]))
        hidden_n = (half_n + half_n * jnp.tanh(half_n)).astype(BF)
        centred_n, scale_n = normed(dot(hidden_n, wno[...]))
        new_nodes[part] = (nodes[part].astype(F32) + centred_n * scale_n).astype(BF)
        for t in range(tiles):
            here = pl.ds(BLOCK * k + TILE * t, TILE)
            sent.append(
                pltpu.make_async_copy(
                    new_nodes.at[here], out_nodes.at[here], out_sems.at[blocks + tiles * k + t]
                )
            )
            sent[-1].start()
    for copy in sent:
        copy.wait()
    for b in range(blocks):
        put_edges(b).wait()


def late(table_at, recv_tile, recv_row, mask, pieces, kept):
    blocks = EDGES // BLOCK
    return pl.pallas_call(
        late_kernel,
        out_shape=[
            jax.ShapeDtypeStruct((NODES, D), BF),
            jax.ShapeDtypeStruct((EDGES, D), BF),
            pltpu.VMEM((EDGES, D), BF),
            pltpu.VMEM((TABLE * PIECES, LANES), F32),
            pltpu.VMEM((NTILE, TILE, D), F32),
        ],
        in_specs=[SMEM, SMEM, VMEM, VMEM] + [ANY] * 6 + [VMEM] * 10,
        out_specs=[ANY, ANY, VMEM, VMEM, VMEM],
        input_output_aliases={11: 2, 12: 3, 13: 4},
        scratch_shapes=[
            pltpu.VMEM((REMOTE, D), BF),
            pltpu.VMEM((2 * BLOCK * PIECES, LANES), F32),
            pltpu.VMEM((NODES, D), BF),
            pltpu.SemaphoreType.DMA((9,)),
            pltpu.SemaphoreType.DMA((blocks + NTILE,)),
        ],
        compiler_params=pltpu.CompilerParams(vmem_limit_bytes=28 << 20),
        cost_estimate=pl.CostEstimate(flops=8 << 30, bytes_accessed=16 << 20, transcendentals=0),
        name="late",
    )(table_at, recv_tile, recv_row, mask, *pieces, *[in_vmem(k) for k in kept])[:2]


def joined_kernel(a, b, out, sems):
    copies = [
        pltpu.make_async_copy(a, out.at[pl.ds(0, TILE)], sems.at[0]),
        pltpu.make_async_copy(b, out.at[pl.ds(TILE, TILE)], sems.at[1]),
    ]
    for copy in copies:
        copy.start()
    for copy in copies:
        copy.wait()


def joined(a, b):
    return pl.pallas_call(
        joined_kernel,
        out_shape=jax.ShapeDtypeStruct((2 * TILE, D), BF),
        in_specs=[ANY, ANY],
        out_specs=VMEM,
        scratch_shapes=[pltpu.SemaphoreType.DMA((2,))],
        compiler_params=pltpu.CompilerParams(vmem_limit_bytes=4 << 20),
        name="joined",
    )(a, b)


def swapped(x, axis, partner):
    return lax.ppermute(x, axis, [(i, partner(i)) for i in range(lax.axis_size(axis))])


def per_device(
    node_latents, edge_latents, senders, receiver_tile, receiver_row, edge_mask, send_map,
    w_edge, w_send, w_recv, w_edge_out, w_node, w_node_agg, w_node_out,
):
    regions = lax.axis_size("region")
    p_z = swapped(first_tile(node_latents), "group", lambda i: i ^ 1)
    coarse, to_inside, to_across, table, node_pre, nodes, recv_proj, ws, we, weo, wna, wno = project(
        send_map, node_latents, w_send, w_recv, w_node, w_edge, w_edge_out, w_node_agg, w_node_out
    )
    inside = swapped(to_inside, "region", lambda i: i ^ 1)
    across = swapped(to_across, "region", lambda i: (i + 1 if i % 2 else i - 1) % regions)
    both = joined(coarse, p_z)
    p_x = [
        swapped(both, "group", lambda i: i ^ 2),
        swapped(both, "group", lambda i: (i + 2 if i // 2 % 2 else i - 2) % 8),
        swapped(both, "group", lambda i: i ^ 4),
    ]
    recv_row = receiver_row.reshape(ETILE, TILE)
    pre, edges, table_at, total = early(
        receiver_tile, recv_row, senders.reshape(ETILE, TILE), edge_latents, recv_proj, we
    )
    return late(
        table_at.reshape(EDGES), receiver_tile, recv_row, edge_mask.reshape(ETILE, TILE),
        [inside, across, p_z] + p_x,
        [pre, edges, table, total, node_pre, nodes, ws, weo, wna, wno],
    )


def solution(mesh):
    by_device = P(("region", "group"))
    rows = P(("region", "group"), None)
    return jax.shard_map(
        per_device,
        mesh=mesh,
        in_specs=(rows, rows) + (by_device,) * 4 + (P(),) * 8,
        out_specs=(rows, rows),
        check_vma=False,
    )
```

```python
import functools

import jax
import jax.numpy as jnp
from jax import lax
from jax.experimental import pallas as pl
from jax.experimental.pallas import tpu as pltpu
from jax.sharding import PartitionSpec as P

TILE = 128
D = 512
NTILE = 8
ETILE = 32
NODES = NTILE * TILE
EDGES = ETILE * TILE
REMOTE = 1536
TABLE = NODES + REMOTE
LANES = 128
PIECES = D // LANES
BLOCK = 512
BF = jnp.bfloat16
F32 = jnp.float32

ANY = pl.BlockSpec(memory_space=pl.ANY)
SMEM = pl.BlockSpec(memory_space=pltpu.SMEM)
VMEM = pl.BlockSpec(memory_space=pltpu.VMEM)


def in_vmem(x):
    return pltpu.with_memory_space_constraint(x, pltpu.VMEM)


def in_hbm(x):
    return pltpu.with_memory_space_constraint(x, pltpu.HBM)


def whole(shape):
    return pl.BlockSpec(shape, lambda i: (0,) * len(shape))


def dot(a, b):
    return jnp.dot(a, b, preferred_element_type=F32)


def normed(centred):
    var = jnp.sum(centred * centred, axis=-1, keepdims=True) * (1.0 / D)
    return centred, lax.rsqrt(var + 1e-05)


def put_rows(table, first, value):
    for c in range(PIECES):
        table[pl.ds(first * PIECES + c, value.shape[0], stride=PIECES), :] = value[
            :, c * LANES : (c + 1) * LANES
        ]


def get_rows(table, first, rows):
    return jnp.concatenate(
        [table[pl.ds(first * PIECES + c, rows, stride=PIECES), :] for c in range(PIECES)], axis=-1
    )


def one_hot(row_of_edge):
    rows = lax.broadcasted_iota(jnp.int32, (TILE, TILE), 0)
    return (rows == row_of_edge).astype(BF)


def first_kernel(nodes, coarse):
    coarse[...] = nodes[...]


def first_tile(node_latents):
    block = pl.BlockSpec((TILE, D), lambda i: (0, 0))
    return pl.pallas_call(
        first_kernel,
        grid=(1,),
        out_shape=jax.ShapeDtypeStruct((TILE, D), BF),
        in_specs=[block],
        out_specs=block,
        compiler_params=pltpu.CompilerParams(vmem_limit_bytes=4 << 20),
        name="first_tile",
    )(in_hbm(node_latents))


def project_kernel(
    send_map, nodes_h, ws_h, wr_h, wn_h, we_h, weo_h, wna_h, wno_h,
    coarse, inside, across, table, node_pre, nodes, recv_proj, ws, we, weo, wna, wno,
    wr, wn, map_s, map_sem, sems, out_sems,
):
    me = lax.axis_index("region") * lax.axis_size("group") + lax.axis_index("group")
    get_map = pltpu.make_async_copy(send_map, map_s, map_sem)
    get_map.start()
    pairs = [
        (nodes_h, nodes), (ws_h, ws), (wr_h, wr), (wn_h, wn), (we_h, we),
        (weo_h, weo), (wna_h, wna), (wno_h, wno),
    ]
    copies = [pltpu.make_async_copy(a, b, sems.at[j]) for j, (a, b) in enumerate(pairs)]
    for copy in copies:
        copy.start()
    get_map.wait()
    copies[0].wait()
    sent = [pltpu.make_async_copy(nodes.at[pl.ds(0, TILE)], coarse, out_sems.at[0])]
    odd = lax.rem(lax.axis_index("region"), 2)
    for k, (side, out) in enumerate(((1 - odd, inside), (odd, across))):
        for j in range(2):
            tile = map_s[side, j, me]
            sent.append(
                pltpu.make_async_copy(
                    nodes.at[pl.ds(pl.multiple_of(tile * TILE, TILE), TILE)],
                    out.at[pl.ds(j * TILE, TILE)],
                    out_sems.at[1 + k * 2 + j],
                )
            )
    for copy in sent:
        copy.start()
    for copy in copies[1:4]:
        copy.wait()
    for k in range(NODES // BLOCK):
        part = slice(BLOCK * k, BLOCK * (k + 1))
        x = nodes[part]
        put_rows(table, BLOCK * k, 0.5 * dot(x, ws[...]).astype(BF).astype(F32))
        recv_proj[part] = dot(x, wr[...]).astype(BF)
        node_pre[part] = dot(x, wn[...])
    for copy in copies[4:] + sent:
        copy.wait()
    for weight in (weo, wno):
        w = weight[...].astype(F32)
        weight[...] = (w - jnp.sum(w, axis=-1, keepdims=True) * (1.0 / D)).astype(BF)


def project(send_map, nodes, w_send, w_recv, w_node, w_edge, w_edge_out, w_node_agg, w_node_out):
    weight = pltpu.VMEM((D, D), BF)
    by_side = jnp.transpose(send_map, (1, 2, 0))
    return pl.pallas_call(
        project_kernel,
        out_shape=[
            jax.ShapeDtypeStruct((TILE, D), BF),
            jax.ShapeDtypeStruct((2 * TILE, D), BF),
            jax.ShapeDtypeStruct((2 * TILE, D), BF),
            pltpu.VMEM((TABLE * PIECES, LANES), F32),
            pltpu.VMEM((NODES, D), F32),
            pltpu.VMEM((NODES, D), BF),
            pltpu.VMEM((NODES, D), BF),
            weight, weight, weight, weight, weight,
        ],
        in_specs=[ANY] * 9,
        out_specs=[ANY] * 3 + [VMEM] * 9,
        scratch_shapes=[
            weight,
            weight,
            pltpu.SMEM(by_side.shape, jnp.int32),
            pltpu.SemaphoreType.DMA,
            pltpu.SemaphoreType.DMA((8,)),
            pltpu.SemaphoreType.DMA((5,)),
        ],
        compiler_params=pltpu.CompilerParams(vmem_limit_bytes=16 << 20),
        cost_estimate=pl.CostEstimate(flops=4 << 30, bytes_accessed=12 << 20, transcendentals=0),
        name="project",
    )(*[in_hbm(v) for v in (by_side, nodes, w_send, w_recv, w_node, w_edge, w_edge_out, w_node_agg, w_node_out)])


def early_kernel(recv_tile, recv_row, senders, edges_h, recv_proj, we, pre, edges, table_at, total, sems):
    blocks = EDGES // BLOCK
    tiles = BLOCK // TILE

    def get(b):
        here = pl.ds(pl.multiple_of(b * BLOCK, BLOCK), BLOCK)
        return pltpu.make_async_copy(edges_h.at[here], edges.at[here], sems.at[b])

    for b in range(blocks):
        get(b).start()
    table_at[...] = senders[...] * PIECES
    total[...] = jnp.zeros_like(total)

    def body(b, _):
        get(b).wait()
        here = pl.ds(pl.multiple_of(b * BLOCK, BLOCK), BLOCK)
        own = dot(edges[here, :], we[...])
        received = []
        for t in range(tiles):
            tile = recv_tile[b * tiles + t]
            hot = one_hot(recv_row[pl.ds(b * tiles + t, 1), :])
            received.append(
                lax.dot_general(
                    hot,
                    recv_proj[pl.ds(pl.multiple_of(tile * TILE, TILE), TILE), :],
                    (((0,), (0,)), ((), ())),
                    preferred_element_type=F32,
                )
            )
        pre[here, :] = 0.5 * (own + jnp.concatenate(received))
        return 0

    lax.fori_loop(0, blocks, body, 0)


def early(recv_tile, recv_row, senders, edges, recv_proj, we):
    return pl.pallas_call(
        early_kernel,
        out_shape=[
            pltpu.VMEM((EDGES, D), F32),
            pltpu.VMEM((EDGES, D), BF),
            jax.ShapeDtypeStruct((ETILE, TILE), jnp.int32),
            pltpu.VMEM((NTILE, TILE, D), F32),
        ],
        in_specs=[SMEM, VMEM, VMEM, ANY, VMEM, VMEM],
        out_specs=[VMEM] * 4,
        scratch_shapes=[pltpu.SemaphoreType.DMA((EDGES // BLOCK,))],
        compiler_params=pltpu.CompilerParams(vmem_limit_bytes=16 << 20),
        cost_estimate=pl.CostEstimate(flops=8 << 30, bytes_accessed=24 << 20, transcendentals=0),
        name="early",
    )(recv_tile, recv_row, senders, in_hbm(edges), in_vmem(recv_proj), in_vmem(we))


def late_kernel(
    table_at, recv_tile, recv_row, mask,
    inside, across, p_z, p_xa, p_xb, p_x2,
    pre, edges_in, table_in, total_in, node_pre, nodes, ws, weo, wna, wno,
    out_nodes, out_edges, edges, table, total,
    remote, picked, new_nodes, sems, out_sems,
):
    tiles = BLOCK // TILE
    blocks = EDGES // BLOCK
    me = lax.axis_index("group")
    panel = [(p_z, me ^ 1)]
    side_x = jnp.where(lax.rem(lax.div(me, 2), 2) == 1, lax.rem(me + 2, 8), lax.rem(me + 6, 8))
    for pair, member in ((p_xa, me ^ 2), (p_xb, side_x), (p_x2, me ^ 4)):
        panel.append((pair.at[pl.ds(0, TILE)], member))
        panel.append((pair.at[pl.ds(TILE, TILE)], member ^ 1))
    odd = lax.rem(lax.axis_index("region"), 2)
    half_at = 2 * TILE
    copies = [
        pltpu.make_async_copy(inside, remote.at[pl.ds(pl.multiple_of((1 - odd) * half_at, half_at), half_at)], sems.at[0]),
        pltpu.make_async_copy(across, remote.at[pl.ds(pl.multiple_of(odd * half_at, half_at), half_at)], sems.at[1]),
    ]
    for j, (piece, member) in enumerate(panel):
        at = pl.multiple_of(4 * TILE + member * TILE, TILE)
        copies.append(pltpu.make_async_copy(piece, remote.at[pl.ds(at, TILE)], sems.at[2 + j]))
    for copy in copies:
        copy.start()

    remote[pl.ds(pl.multiple_of(4 * TILE + me * TILE, TILE), TILE), :] = nodes[0:TILE, :]
    live = jnp.sum(mask[...])
    for copy in copies:
        copy.wait()
    for k in range(REMOTE // BLOCK):
        proj = dot(remote[BLOCK * k : BLOCK * (k + 1)], ws[...])
        put_rows(table, NODES + BLOCK * k, 0.5 * proj.astype(BF).astype(F32))

    def put_edges(b):
        here = pl.ds(pl.multiple_of(b * BLOCK, BLOCK), BLOCK)
        return pltpu.make_async_copy(edges.at[here], out_edges.at[here], out_sems.at[b])

    def take(b, slot, start, stop):
        first = pl.multiple_of(b * BLOCK, BLOCK)
        for e in range(start, stop):
            to = (slot * BLOCK + e) * PIECES
            picked[to : to + PIECES, :] = table[pl.ds(pl.multiple_of(table_at[first + e], PIECES), PIECES), :]

    def edge_block(b, slot, b_next):
        first = pl.multiple_of(b * BLOCK, BLOCK)
        here = pl.ds(first, BLOCK)
        half = pre[here, :] + get_rows(picked, slot * BLOCK, BLOCK)
        hidden = (half + half * jnp.tanh(half)).astype(BF)
        out = dot(hidden, weo[...])
        parts = []
        for p in range(0, BLOCK, 32):
            take(b_next, 1 - slot, p, p + 32)
            centred, scale = normed(out[p : p + 32])
            slots = lax.broadcasted_iota(jnp.int32, (32, 1), 0) + (first + p)
            message = centred * jnp.where(slots < live, scale, 0.0)
            there = pl.ds(pl.multiple_of(first + p, 32), 32)
            edges[there, :] = (edges[there, :].astype(F32) + message).astype(BF)
            parts.append(message.astype(BF))
        put_edges(b).start()
        rounded = jnp.concatenate(parts)
        for t in range(tiles):
            hot = one_hot(recv_row[pl.ds(b * tiles + t, 1), :])
            total[recv_tile[b * tiles + t]] += dot(hot, rounded[t * TILE : (t + 1) * TILE])

    take(0, 0, 0, BLOCK)

    def body(j, _):
        edge_block(2 * j, 0, 2 * j + 1)
        edge_block(2 * j + 1, 1, jnp.minimum(2 * j + 2, blocks - 1))
        return 0

    lax.fori_loop(0, blocks // 2, body, 0)
    sent = []
    for k in range(NODES // BLOCK):
        part = slice(BLOCK * k, BLOCK * (k + 1))
        summed = total[tiles * k : tiles * (k + 1)].reshape(BLOCK, D).astype(BF)
        half_n = 0.5 * (node_pre[part] + dot(summed, wna[...]))
        hidden_n = (half_n + half_n * jnp.tanh(half_n)).astype(BF)
        centred_n, scale_n = normed(dot(hidden_n, wno[...]))
        new_nodes[part] = (nodes[part].astype(F32) + centred_n * scale_n).astype(BF)
        for t in range(tiles):
            here = pl.ds(BLOCK * k + TILE * t, TILE)
            sent.append(
                pltpu.make_async_copy(
                    new_nodes.at[here], out_nodes.at[here], out_sems.at[blocks + tiles * k + t]
                )
            )
            sent[-1].start()
    for copy in sent:
        copy.wait()
    for b in range(blocks):
        put_edges(b).wait()


def late(table_at, recv_tile, recv_row, mask, pieces, kept):
    blocks = EDGES // BLOCK
    return pl.pallas_call(
        late_kernel,
        out_shape=[
            jax.ShapeDtypeStruct((NODES, D), BF),
            jax.ShapeDtypeStruct((EDGES, D), BF),
            pltpu.VMEM((EDGES, D), BF),
            pltpu.VMEM((TABLE * PIECES, LANES), F32),
            pltpu.VMEM((NTILE, TILE, D), F32),
        ],
        in_specs=[SMEM, SMEM, VMEM, VMEM] + [ANY] * 6 + [VMEM] * 10,
        out_specs=[ANY, ANY, VMEM, VMEM, VMEM],
        input_output_aliases={11: 2, 12: 3, 13: 4},
        scratch_shapes=[
            pltpu.VMEM((REMOTE, D), BF),
            pltpu.VMEM((2 * BLOCK * PIECES, LANES), F32),
            pltpu.VMEM((NODES, D), BF),
            pltpu.SemaphoreType.DMA((9,)),
            pltpu.SemaphoreType.DMA((blocks + NTILE,)),
        ],
        compiler_params=pltpu.CompilerParams(vmem_limit_bytes=28 << 20),
        cost_estimate=pl.CostEstimate(flops=8 << 30, bytes_accessed=16 << 20, transcendentals=0),
        name="late",
    )(table_at, recv_tile, recv_row, mask, *pieces, *[in_vmem(k) for k in kept])[:2]


def joined_kernel(a, b, inside_in, across_in, out, inside, across, sems):
    copies = [
        pltpu.make_async_copy(a, out.at[pl.ds(0, TILE)], sems.at[0]),
        pltpu.make_async_copy(b, out.at[pl.ds(TILE, TILE)], sems.at[1]),
        pltpu.make_async_copy(inside_in, inside, sems.at[2]),
        pltpu.make_async_copy(across_in, across, sems.at[3]),
    ]
    for copy in copies:
        copy.start()
    for copy in copies:
        copy.wait()


def joined(a, b, inside, across):
    return pl.pallas_call(
        joined_kernel,
        out_shape=[jax.ShapeDtypeStruct((2 * TILE, D), BF)] * 3,
        in_specs=[ANY] * 4,
        out_specs=[VMEM] * 3,
        scratch_shapes=[pltpu.SemaphoreType.DMA((4,))],
        compiler_params=pltpu.CompilerParams(vmem_limit_bytes=4 << 20),
        name="joined",
    )(a, b, inside, across)


def swapped(x, axis, partner):
    return lax.ppermute(x, axis, [(i, partner(i)) for i in range(lax.axis_size(axis))])


def per_device(
    node_latents, edge_latents, senders, receiver_tile, receiver_row, edge_mask, send_map,
    w_edge, w_send, w_recv, w_edge_out, w_node, w_node_agg, w_node_out,
):
    regions = lax.axis_size("region")
    p_z = swapped(first_tile(node_latents), "group", lambda i: i ^ 1)
    coarse, to_inside, to_across, table, node_pre, nodes, recv_proj, ws, we, weo, wna, wno = project(
        send_map, node_latents, w_send, w_recv, w_node, w_edge, w_edge_out, w_node_agg, w_node_out
    )
    both, to_inside, to_across = joined(coarse, p_z, to_inside, to_across)
    inside = swapped(to_inside, "region", lambda i: i ^ 1)
    across = swapped(to_across, "region", lambda i: (i + 1 if i % 2 else i - 1) % regions)
    p_x = [
        swapped(both, "group", lambda i: i ^ 2),
        swapped(both, "group", lambda i: (i + 2 if i // 2 % 2 else i - 2) % 8),
        swapped(both, "group", lambda i: i ^ 4),
    ]
    recv_row = receiver_row.reshape(ETILE, TILE)
    pre, edges, table_at, total = early(
        receiver_tile, recv_row, senders.reshape(ETILE, TILE), edge_latents, recv_proj, we
    )
    return late(
        table_at.reshape(EDGES), receiver_tile, recv_row, edge_mask.reshape(ETILE, TILE),
        [inside, across, p_z] + p_x,
        [pre, edges, table, total, node_pre, nodes, ws, weo, wna, wno],
    )


def solution(mesh):
    by_device = P(("region", "group"))
    rows = P(("region", "group"), None)
    return jax.shard_map(
        per_device,
        mesh=mesh,
        in_specs=(rows, rows) + (by_device,) * 4 + (P(),) * 8,
        out_specs=(rows, rows),
        check_vma=False,
    )
```
